32 devices in a mesh: slab: 8 (over z, x), freq: 4 (over y, core).
Axes of the slice: x: 2, y: 2, z: 4, core: 2. Of those that a mesh axis runs over, the one named last changes fastest.
Arguments:
- source: bfloat16 [4, 2, 3, 64, 64, 128], P('freq', None, None, 'slab'), may hold values from -6 to 6
- omega: float32 [4], P('freq'), may hold values from 0.2 to 5
- sigma_blocks: float32 [256], replicated, may hold values from 0.25 to 4
- block_ids: int32 [64, 64, 128], P('slab'), may hold values from 0 to 255
- rec_owner: int32 [1024, 1], P('slab'), may hold values from 0 to 7; in each aligned block of 128 rows (0 to 127, 128 to 255, ...) at most 32 rows name the same one
- rec_edge: int32 [1024], P('slab'), may hold values from 0 to 196607
- observed: float32 [4, 2, 1024], P('freq', None, 'slab'), may hold values from -4 to 4
Outputs:
- forward_field: float32 [4, 2, 3, 64, 64, 128], P('freq', None, None, 'slab')
- adjoint_field: float32 [4, 2, 3, 64, 64, 128], P('freq', None, None, 'slab')
- gradient: float32 [256], replicated
The draws below stay inside these ranges and needn't reach their ends.
Inputs may be any that keep to these rules, and one draw needn't show every extreme that they name: `rec_owner`: among the receiver rows of one slab device no slab is named more than 32 times; in some device's rows one slab is named exactly 32 times.
All inputs are finite; a program needn't handle non-finite values.
Results may differ from the reference program's by a relative error of at most 0.0003.
Values sent between devices are 32-bit elements; how exact they have to be, the bound alone decides.
A program may use at most 256 MiB of HBM per device.

```python
import math
import jax
import jax.numpy as jnp
import numpy as np
from jax import lax

CX = 8
NY = 64
NZ = 128
SWEEPS = 4
REC_DEV = 128
BLK_REG = 32
CAP = 32
NX = 64
NPAIR = 4
NREC = 1024
NBLK = 256
EDGES = 196608
N_SLAB = 8


def draw_block_ids(key, part):
    plane_index = jnp.arange(NX, dtype=jnp.int32)[:, None, None]
    region = (plane_index + CX // 2) // CX % N_SLAB
    inner_block = jax.random.randint(key, (NX, NY, NZ), 0, BLK_REG, dtype=jnp.int32)
    return (region * BLK_REG + inner_block).astype(jnp.int32)


def set_ends(values, own_key, least, top_value):
    dims = values.shape
    index_at = [jax.random.randint(jax.random.fold_in(own_key, axis), (), 0, dims[axis]) for axis in range(len(dims))]
    values = values.at[tuple(index_at)].set(least)
    longest = dims.index(max(dims))
    index_at[longest] = (index_at[longest] + 1) % dims[longest]
    return values.at[tuple(index_at)].set(top_value)


def level_of(rng, extent, pieces, smallest, high):
    loudness, own = 1.0, jax.random.fold_in(rng, 6)
    for position, shards_of in pieces:
        draws = jnp.exp(jax.random.uniform(jax.random.fold_in(own, position), (shards_of,), jnp.float32, smallest / len(pieces), high / len(pieces)))
        loudness = loudness * jnp.repeat(draws, extent[position] // shards_of).reshape([-1 if axis == position else 1 for axis in range(len(extent))])
    return loudness


def deal_out(key, own, number, rows, count, top, bound, skew):
    order = jax.random.permutation(key, count)
    heavy_load, common = shares(count, rows * top, bound, skew, True), shares(count, rows * top, bound, skew, False)
    places = jnp.arange(count)

    def named(tallies, offset_by):
        used = int((tallies > 0).sum())
        fixed = max(1, used // 4)
        shifted = fixed + (places - fixed + offset_by * (used - fixed)) % max(1, count - fixed)
        return jnp.zeros((count,), jnp.int32).at[order[jnp.where(places < fixed, places, shifted)]].set(jnp.asarray(tallies, jnp.int32))

    tallies = jnp.where(number % 4 == 0, named(heavy_load, number // 4), named(common, number - number // 4 - 1))
    mixed = jax.random.permutation(jax.random.fold_in(own, 3), count)
    source_of, sink = mixed[0:count // 2 * 2:2], mixed[1:count // 2 * 2:2]
    margin = jnp.minimum(tallies[source_of] - 1, bound - tallies[sink]) // 2
    margin = jnp.where((source_of == order[0]) | (sink == order[0]) | (tallies[sink] == 0), 0, jnp.maximum(margin, 0))
    shifted = jax.random.randint(jax.random.fold_in(own, 4), (count // 2,), 0, 1 << 20) % (margin + 1)
    tallies = tallies.at[source_of].add(-shifted).at[sink].add(shifted)
    members = jnp.searchsorted(jnp.cumsum(tallies), jnp.arange(rows * top), side="right").astype(jnp.int32)
    grid = members.reshape(top, rows).T
    grid = grid[jax.random.permutation(jax.random.fold_in(own, 1), rows)]
    offset_by = jax.random.randint(jax.random.fold_in(own, 2), (rows, 1), 0, top)
    return jnp.take_along_axis(grid, (jnp.arange(top)[None, :] + offset_by) % top, axis=1)


def shares(number_of, total, most, slope, full):
    portions = [(1 << 20) // math.isqrt(grade ** slope) + 1 for grade in range(1, number_of + 1)]
    largest = most if full else min(most, max(-(-total // number_of), total * portions[0] // sum(portions)))
    least = 1 if total - largest >= number_of - 1 else 0
    counts, surplus = [largest] + [least] * (number_of - 1), total - largest - least * (number_of - 1)
    while surplus > 0:
        movable = [i for i in range(1, number_of) if counts[i] < largest] or [i for i in range(1, number_of) if counts[i] < most]
        whole, remaining = sum([portions[i] for i in movable]), surplus
        for i in movable:
            addition = min(most - counts[i], max(1, remaining * portions[i] // whole), surplus)
            counts[i] = counts[i] + addition
            surplus = surplus - addition
    return np.array(counts)


def bell_draw(stream_key, dims, spread, reach, split=(), kind=jnp.bfloat16):
    entries = spread * jax.random.normal(stream_key, dims, jnp.float32)
    if split:
        entries = entries * level_of(stream_key, dims, split, -0.22, 0.18)
    return jnp.clip(entries, -reach, reach).astype(kind)


def setup_inputs(seed: int = 0) -> dict:
    streams_of = jax.random.split(jax.random.key(seed), 8)
    source = bell_draw(streams_of[0], (NPAIR, 2, 3, NX, NY, NZ), 1.0, 6.0, ((0, 4), (3, 8)))
    omega = jnp.clip(jnp.exp(math.log(5.0) - 3.218876 * jax.random.uniform(streams_of[1], (NPAIR,), jnp.float32) ** level_of(streams_of[1], (NPAIR,), ((0, 4),), -0.2, 0.2)), 0.2, 5.0)
    sigma_blocks = jnp.clip(jnp.exp(jax.random.uniform(streams_of[2], (NBLK,), jnp.float32, math.log(0.25), math.log(4.0))), 0.25, 4.0)
    block_ids = draw_block_ids(jax.random.fold_in(streams_of[7], 71), 0)
    rec_owner_keys = jax.random.split(jax.random.fold_in(streams_of[4], 1), NREC // REC_DEV)
    rec_owner_turns = jax.random.permutation(jax.random.fold_in(streams_of[4], 3), NREC // REC_DEV)
    rec_owner = jax.vmap(lambda own, number: deal_out(jax.random.fold_in(streams_of[4], 2), own, number, REC_DEV, N_SLAB, 1, CAP, 2))(rec_owner_keys, rec_owner_turns).reshape((NREC, 1))
    rec_edge = set_ends(jax.random.randint(streams_of[5], (NREC,), 0, EDGES), jax.random.fold_in(streams_of[5], 1), 0, EDGES - 1).astype(jnp.int32)
    observed = bell_draw(streams_of[6], (NPAIR, 2, NREC), 0.3, 4.0, ((0, 4), (2, 8)), jnp.float32)
    return dict(source=source, omega=omega, sigma_blocks=sigma_blocks, block_ids=block_ids, rec_owner=rec_owner, rec_edge=rec_edge, observed=observed)


epsilon = 1e-6


def forward_diff(values, along):
    along = along % values.ndim
    count = values.shape[along]
    ahead_values = jnp.concatenate([lax.slice_in_dim(values, 1, count, axis=along), jnp.zeros_like(lax.slice_in_dim(values, 0, 1, axis=along))], axis=along)
    return ahead_values - values


def adjoint_diff(values, along):
    along = along % values.ndim
    count = values.shape[along]
    behind = jnp.concatenate([jnp.zeros_like(lax.slice_in_dim(values, 0, 1, axis=along)), lax.slice_in_dim(values, 0, count - 1, axis=along)], axis=along)
    return behind - values


def curl_curl(field):
    edge_first = field[..., 0, :, :, :]
    edge_second = field[..., 1, :, :, :]
    edge_third = field[..., 2, :, :, :]
    curl_first = forward_diff(edge_third, -2) - forward_diff(edge_second, -1)
    curl_second = forward_diff(edge_first, -1) - forward_diff(edge_third, -3)
    curl_third = forward_diff(edge_second, -3) - forward_diff(edge_first, -2)
    back_first = adjoint_diff(curl_second, -1) - adjoint_diff(curl_third, -2)
    back_second = adjoint_diff(curl_third, -3) - adjoint_diff(curl_first, -1)
    back_third = adjoint_diff(curl_first, -2) - adjoint_diff(curl_second, -3)
    return jnp.stack([back_first, back_second, back_third], axis=-4)


def residual_sweeps(right_side, damping):
    denominator = 16.0 + damping * damping
    residual = right_side
    solution = jnp.zeros_like(right_side)
    for iteration in range(SWEEPS):
        residual_real = residual[0]
        residual_imag = residual[1]
        precond_real = (4.0 * residual_real + damping * residual_imag) / denominator
        precond_imag = (4.0 * residual_imag - damping * residual_real) / denominator
        stiffness = curl_curl(jnp.stack([precond_real, precond_imag]))
        image_real = stiffness[0] - damping * precond_imag
        image_imag = stiffness[1] + damping * precond_real
        upper_real = jnp.sum(image_real * residual_real + image_imag * residual_imag)
        upper_imag = jnp.sum(image_real * residual_imag - image_imag * residual_real)
        lower_sum = jnp.sum(image_real * image_real + image_imag * image_imag) + epsilon
        step_real = upper_real / lower_sum
        step_imag = upper_imag / lower_sum
        solution = solution + jnp.stack([step_real * precond_real - step_imag * precond_imag, step_real * precond_imag + step_imag * precond_real])
        residual = residual - jnp.stack([step_real * image_real - step_imag * image_imag, step_real * image_imag + step_imag * image_real])
    return solution


def reference(source, omega, sigma_blocks, block_ids, rec_owner, rec_edge, observed):
    conductivity = jnp.take(sigma_blocks, block_ids, axis=0)
    component = rec_edge // (CX * NY * NZ)
    remainder = rec_edge % (CX * NY * NZ)
    plane_index = remainder // (NY * NZ)
    inside = remainder % (NY * NZ)
    global_edge = (component * (NX * NY * NZ) + (rec_owner[:, 0] * CX + plane_index) * (NY * NZ) + inside).astype(jnp.int32)

    def per_pair(inputs):
        right_side, frequency, measured = inputs
        damping = frequency * conductivity
        forward_field = residual_sweeps(right_side.astype(jnp.float32), damping)
        flat_field = forward_field.reshape(2, -1)
        predicted = jnp.take(flat_field, global_edge, axis=1)
        misfit = predicted - measured
        adjoint_flat = jnp.zeros_like(flat_field).at[0, global_edge].add(misfit[0]).at[1, global_edge].add(-misfit[1])
        adjoint_field = residual_sweeps(adjoint_flat.reshape(forward_field.shape), damping)
        cell_term = frequency * jnp.sum(adjoint_field[0] * forward_field[1] + adjoint_field[1] * forward_field[0], axis=0)
        block_term = jax.ops.segment_sum(cell_term.reshape(-1), block_ids.reshape(-1), num_segments=BLK_REG * N_SLAB)
        return forward_field, adjoint_field, block_term

    forward_field, adjoint_field, pair_terms = lax.map(per_pair, (source, omega, observed))
    return forward_field, adjoint_field, jnp.sum(pair_terms, axis=0)
```

```python
import functools

import jax
import jax.numpy as jnp
from jax import lax
from jax.experimental import pallas as pl
from jax.experimental.pallas import tpu as pltpu
from jax.sharding import PartitionSpec as P

SWEEPS = 4
EPSILON = 1e-06
LOW = 16
MESH = pl.DeviceIdType.MESH
F32 = jnp.float32
BF16 = jnp.bfloat16
PAIRS = [(i, j) for i in range(SWEEPS + 1) for j in range(i, SWEEPS + 1) if j > 0]


def lookup_kernel(omega_ref, sigma_ref, ids_ref, real_ref, imag_ref):
    planes, rows, lanes = ids_ref.shape
    tables = [jnp.broadcast_to(sigma_ref[k : k + 1, :], (8, lanes)) for k in range(sigma_ref.shape[0])]
    omega = omega_ref[0]
    per = rows // 8

    def step(i, carry):
        x, y = i // per, pl.multiple_of(i % per * 8, 8)
        ids = ids_ref[x, pl.ds(y, 8), :]
        low, high = ids & (lanes - 1), ids >> 7
        value = jnp.take_along_axis(tables[0], low, axis=1)
        for k in range(1, len(tables)):
            value = jnp.where(high == k, jnp.take_along_axis(tables[k], low, axis=1), value)
        damping = omega * value
        inverse = 1.0 / (16.0 + damping * damping)
        real_ref[x, pl.ds(y, 8), :] = 4.0 * inverse
        imag_ref[x, pl.ds(y, 8), :] = damping * inverse
        return carry

    lax.fori_loop(0, planes * per, step, 0, unroll=4)


def split(values):
    high = values.astype(BF16)
    return high, (values - high.astype(F32)).astype(BF16)


def kernel(
    n, nf, high_blocks,
    omega_ref, source_ref, real_ref, imag_ref, ids_ref, pack_ref,
    forward_ref, adjoint_ref, gradient_ref,
    basis, zb, curl, up_out, down_out, low_in, high_in,
    gram_out, gram_in, pack_in, grad_out, grad_in, grad_out2, grad_in2,
    rows_hot, rows_hot_t, field_hi, field_lo, mis_hi, mis_lo, acc,
    up_s, up_r, down_s, down_r, gram_s, gram_r, pack_s, pack_r, grad_s, grad_r, grad2_s, grad2_r,
):
    me = lax.axis_index("slab")
    mine = lax.axis_index("freq")
    planes, rows, lanes = real_ref.shape
    last = planes - 1
    cells_rows = 3 * planes * rows

    barrier = pltpu.get_barrier_semaphore()
    for d in range(1, n):
        pl.semaphore_signal(barrier, inc=1, device_id={"slab": lax.rem(me + d, n)}, device_id_type=MESH)
    for d in range(1, nf):
        pl.semaphore_signal(barrier, inc=1, device_id={"freq": lax.rem(mine + d, nf)}, device_id_type=MESH)
    pl.semaphore_wait(barrier, n + nf - 2)

    def spread(src, dst, send, recv, axis, count, position):
        copies = []
        for d in range(1, count):
            copy = pltpu.make_async_remote_copy(
                src_ref=src, dst_ref=dst.at[d], send_sem=send.at[d], recv_sem=recv.at[d],
                device_id={axis: lax.rem(position + d, count)}, device_id_type=MESH,
            )
            copy.start()
            copies.append(copy)
        return copies

    def total_of(own, buffer, count, position):
        buffer[0] = own
        total = jnp.zeros(own.shape, F32)
        for p in range(count):
            total = total + buffer[lax.rem(position - p + count, count)]
        return total

    lane = lax.broadcasted_iota(jnp.int32, (rows, lanes), 1)
    row = lax.broadcasted_iota(jnp.int32, (rows, lanes), 0)

    def f3(v):
        return jnp.where(lane == lanes - 1, 0.0, pltpu.roll(v, lanes - 1, 1)) - v

    def g3(v):
        return jnp.where(lane == 0, 0.0, pltpu.roll(v, 1, 1)) - v

    def f2(v):
        return jnp.where(row == rows - 1, 0.0, pltpu.roll(v, rows - 1, 0)) - v

    def g2(v):
        return jnp.where(row == 0, 0.0, pltpu.roll(v, 1, 0)) - v

    packs = spread(pack_ref, pack_in, pack_s, pack_r, "slab", n, me)
    pack_in[0] = pack_ref[...]
    valid = jnp.where(me > 0, 1.0, 0.0).astype(F32)

    def precondition(t, x):
        mr, mi = real_ref[x], imag_ref[x]
        for comp in range(3):
            br, bi = basis[t, 0, comp, x], basis[t, 1, comp, x]
            zb[0, comp, x] = mr * br + mi * bi
            zb[1, comp, x] = mr * bi - mi * br

    def up_copy(slot):
        return pltpu.make_async_remote_copy(
            src_ref=up_out.at[slot], dst_ref=low_in.at[slot], send_sem=up_s.at[slot],
            recv_sem=up_r.at[slot], device_id={"slab": lax.rem(me + 1, n)}, device_id_type=MESH,
        )

    def down_copy(slot):
        return pltpu.make_async_remote_copy(
            src_ref=down_out.at[slot], dst_ref=high_in.at[slot], send_sem=down_s.at[slot],
            recv_sem=down_r.at[slot], device_id={"slab": lax.rem(me + n - 1, n)}, device_id_type=MESH,
        )

    def plane(t, c, x, e2n, e3n, b2p, b3p):
        e1, e2, e3 = zb[c, 0, x], zb[c, 1, x], zb[c, 2, x]
        b1 = f2(e3) - f3(e2)
        b2 = f3(e1) - (e3n - e3)
        b3 = e2n - e2 - f2(e1)
        curl[c, 0, x], curl[c, 1, x] = b2, b3
        basis[t + 1, c, 0, x] = g3(b2) - g2(b3) - 4.0 * e1 + basis[t, c, 0, x]
        basis[t + 1, c, 1, x] = b3p - b3 - g3(b1) - 4.0 * e2 + basis[t, c, 1, x]
        basis[t + 1, c, 2, x] = g2(b1) - (b2p - b2) - 4.0 * e3 + basis[t, c, 2, x]

    def apply(first, t):
        slot = first + t
        precondition(t, 0)
        for c in range(2):
            down_out[slot, c, 0] = zb[c, 1, 0]
            down_out[slot, c, 1] = zb[c, 2, 0]

        @pl.when(me > 0)
        def _():
            down_copy(slot).start()

        precondition(t, last)
        for c in range(2):
            up_out[slot, c, 0] = f3(zb[c, 0, last]) + zb[c, 2, last]
            up_out[slot, c, 1] = f2(zb[c, 0, last]) + zb[c, 1, last]

        @pl.when(me < n - 1)
        def _():
            up_copy(slot).start()

        def inner(x, carry):
            precondition(t, x)
            return carry

        lax.fori_loop(1, last, inner, 0)
        for c in range(2):
            curl[c, 0, 0] = f3(zb[c, 0, 0]) - (zb[c, 2, 1] - zb[c, 2, 0])
            curl[c, 1, 0] = zb[c, 1, 1] - zb[c, 1, 0] - f2(zb[c, 0, 0])

        def middle(x, carry):
            for c in range(2):
                plane(t, c, x, zb[c, 1, x + 1], zb[c, 2, x + 1], curl[c, 0, x - 1], curl[c, 1, x - 1])
            return carry

        lax.fori_loop(1, last, middle, 0)

        @pl.when(me > 0)
        def _():
            up_copy(slot).wait_recv()
            down_copy(slot).wait_send()

        @pl.when(me == 0)
        def _():
            low_in[slot] = jnp.zeros(low_in.shape[1:], F32)

        for c in range(2):
            plane(
                t, c, 0, zb[c, 1, 1], zb[c, 2, 1],
                (low_in[slot, c, 0] - zb[c, 2, 0]) * valid,
                (zb[c, 1, 0] - low_in[slot, c, 1]) * valid,
            )

        @pl.when(me < n - 1)
        def _():
            down_copy(slot).wait_recv()
            up_copy(slot).wait_send()

        @pl.when(me == n - 1)
        def _():
            high_in[slot] = jnp.zeros(high_in.shape[1:], F32)

        for c in range(2):
            plane(
                t, c, last, high_in[slot, c, 0], high_in[slot, c, 1],
                curl[c, 0, last - 1], curl[c, 1, last - 1],
            )

    per = rows // 8

    def solve(which, out_ref):
        def sweep(t, carry):
            apply(which * SWEEPS, t)
            return carry

        lax.fori_loop(0, SWEEPS, sweep, 0)

        def products(i, sums):
            x, y = i // per, pl.multiple_of(i % per * 8, 8)
            sums = list(sums)
            for comp in range(3):
                re = [basis[k, 0, comp, x, pl.ds(y, 8), :] for k in range(SWEEPS + 1)]
                im = [basis[k, 1, comp, x, pl.ds(y, 8), :] for k in range(SWEEPS + 1)]
                at = 0
                for i_, j_ in PAIRS:
                    sums[at] = sums[at] + (re[i_] * re[j_] + im[i_] * im[j_])
                    at += 1
                    if i_ != j_:
                        sums[at] = sums[at] + (re[i_] * im[j_] - im[i_] * re[j_])
                        at += 1
            return tuple(sums)

        count = gram_out.shape[1]
        zero = jnp.zeros((8, lanes), F32)
        sums = lax.fori_loop(0, planes * per, products, (zero,) * count)
        for k in range(count):
            gram_out[which, k : k + 1, :] = jnp.sum(sums[k], axis=0, keepdims=True)
        copies = spread(gram_out.at[which], gram_in.at[which], gram_s.at[which], gram_r.at[which], "slab", n, me)
        for copy in copies:
            copy.wait()
        total = total_of(gram_out[which], gram_in.at[which], n, me)
        total = jnp.broadcast_to(jnp.sum(total, axis=1, keepdims=True), total.shape)
        gram, at = {}, 0
        for i, j in PAIRS:
            re = total[at : at + 1, :]
            at += 1
            im = jnp.zeros_like(re)
            if i != j:
                im = total[at : at + 1, :]
                at += 1
            gram[i, j] = (re, im)
            gram[j, i] = (re, -im)
        one = jnp.ones((1, lanes), F32)
        none = jnp.zeros((1, lanes), F32)

        def times(a, b):
            return a[0] * b[0] - a[1] * b[1], a[0] * b[1] + a[1] * b[0]

        poly = [(one, none)]
        coef = [(none, none) for _ in range(SWEEPS)]
        for k in range(SWEEPS):
            up = (none, none)
            below = none
            for i in range(k + 1):
                conj = (poly[i][0], -poly[i][1])
                for j in range(k + 1):
                    both = times(conj, poly[j])
                    term = times(both, gram[i + 1, j])
                    up = (up[0] + term[0], up[1] + term[1])
                    below = below + times(both, gram[i + 1, j + 1])[0]
            below = below + EPSILON
            step = (up[0] / below, up[1] / below)
            moved = [times(step, p) for p in poly]
            for i in range(k + 1):
                coef[i] = (coef[i][0] + moved[i][0], coef[i][1] + moved[i][1])
            grown = poly + [(none, none)]
            for i in range(k + 1):
                grown[i + 1] = (grown[i + 1][0] - moved[i][0], grown[i + 1][1] - moved[i][1])
            poly = grown

        wide = [(jnp.broadcast_to(a, (rows, lanes)), jnp.broadcast_to(b, (rows, lanes))) for a, b in coef]

        def combine(x, carry):
            mr, mi = real_ref[x], imag_ref[x]
            for comp in range(3):
                sr = jnp.zeros((rows, lanes), F32)
                si = jnp.zeros((rows, lanes), F32)
                for k in range(SWEEPS):
                    br, bi = basis[k, 0, comp, x], basis[k, 1, comp, x]
                    sr = sr + (wide[k][0] * br - wide[k][1] * bi)
                    si = si + (wide[k][0] * bi + wide[k][1] * br)
                out_ref[0, comp, x] = mr * sr + mi * si
                out_ref[1, comp, x] = mr * si - mi * sr
            return carry

        lax.fori_loop(0, planes, combine, 0)

    def load(x, carry):
        for c in range(2):
            for comp in range(3):
                basis[0, c, comp, x] = source_ref[c, comp, x].astype(F32)
        return carry

    lax.fori_loop(0, planes, load, 0)
    solve(0, forward_ref)

    for copy in packs:
        copy.wait()
    self_id = me.astype(F32)
    blocks = cells_rows // lanes
    for comp in range(3):
        for c in range(2):
            hi, lo = split(forward_ref[c, comp].reshape(planes * rows, lanes))
            where = (slice(comp * planes * rows, (comp + 1) * planes * rows), slice(c * lanes, (c + 1) * lanes))
            field_hi[where] = hi
            field_lo[where] = lo

    lane_sq = lax.broadcasted_iota(jnp.int32, (lanes, lanes), 1).astype(F32)
    row_sq = lax.broadcasted_iota(jnp.int32, (lanes, lanes), 0).astype(F32)

    def receivers(d, carry):
        pack = pack_in[d]
        at = pl.ds(pl.multiple_of(d * lanes, lanes), lanes)
        owned = jnp.where(pack[0:1, :] == self_id, pack[1:2, :], -1.0)
        owned = jnp.concatenate([owned, pack[2:8, :], owned], axis=0)
        column = jnp.concatenate([owned] * (lanes // 8), axis=0).T
        place = column[:, 0:1]
        for k in range(blocks):
            rows_hot[:, k * lanes : (k + 1) * lanes] = jnp.where(
                lane_sq == place - float(k * lanes), 1.0, 0.0
            ).astype(BF16)
            rows_hot_t[k * lanes : (k + 1) * lanes, at] = jnp.where(
                row_sq == owned[0:1, :] - float(k * lanes), 1.0, 0.0
            ).astype(BF16)
        picked = jnp.dot(rows_hot[...], field_hi[...], preferred_element_type=F32)
        picked = picked + jnp.dot(rows_hot[...], field_lo[...], preferred_element_type=F32)
        here = lane_sq == column[:, 1:2]
        re = jnp.where(here, picked[:, :lanes] - column[:, 2:3], 0.0)
        im = jnp.where(here, column[:, 3:4] - picked[:, lanes:], 0.0)
        for part, values in enumerate((re, im)):
            hi, lo = split(values)
            mis_hi[at, part * lanes : (part + 1) * lanes] = hi
            mis_lo[at, part * lanes : (part + 1) * lanes] = lo
        return carry

    lax.fori_loop(0, n, receivers, 0)
    group = 4
    for comp in range(3):
        for x in range(0, planes, group):
            begin = (comp * planes + x) * rows
            hot = rows_hot_t[begin : begin + group * rows, :]
            added = jnp.dot(hot, mis_hi[...], preferred_element_type=F32)
            added = added + jnp.dot(hot, mis_lo[...], preferred_element_type=F32)
            for c in range(2):
                basis[0, c, comp, x : x + group] = added[:, c * lanes : (c + 1) * lanes].reshape(
                    group, rows, lanes
                )

    solve(1, adjoint_ref)

    omega = omega_ref[0]
    high_iota = lax.broadcasted_iota(jnp.int32, (high_blocks, lanes), 0)
    low_iota = lax.broadcasted_iota(jnp.int32, (LOW, lanes), 0)
    acc[...] = jnp.zeros(acc.shape, F32)
    chunks = rows // 16

    def cells(i, carry):
        x, y = i // chunks, pl.multiple_of(i % chunks * 16, 16)
        value = jnp.zeros((16, lanes), F32)
        for comp in range(3):
            fr, fi = forward_ref[0, comp, x, pl.ds(y, 16), :], forward_ref[1, comp, x, pl.ds(y, 16), :]
            ar, ai = adjoint_ref[0, comp, x, pl.ds(y, 16), :], adjoint_ref[1, comp, x, pl.ds(y, 16), :]
            value = value + (ar * fi + ai * fr)
        value = omega * value
        ids = ids_ref[x, pl.ds(y, 16), :]
        high, low = ids >> 4, ids & (LOW - 1)
        hot = jnp.concatenate(
            [jnp.where(high[r : r + 1, :] == high_iota, 1.0, 0.0) for r in range(16)], axis=0
        ).astype(BF16)
        spot = jnp.concatenate(
            [jnp.where(low[r : r + 1, :] == low_iota, value[r : r + 1, :], 0.0) for r in range(16)], axis=0
        )
        for piece in split(spot):
            acc[...] += lax.dot_general(
                hot, piece, (((1,), (1,)), ((), ())), preferred_element_type=F32
            )
        return carry

    lax.fori_loop(0, planes * chunks, cells, 0)
    wide_lane = lax.broadcasted_iota(jnp.int32, (high_blocks, 16 * LOW), 1)
    diagonal = jnp.zeros((high_blocks, 16 * LOW), F32)
    for r in range(16):
        inside = (wide_lane >= r * LOW) & (wide_lane < (r + 1) * LOW)
        diagonal = diagonal + jnp.where(inside, acc[r * high_blocks : (r + 1) * high_blocks, :], 0.0)
    folded = diagonal[:, :lanes] + diagonal[:, lanes:]
    for shift in (64, 32, 16):
        folded = folded + pltpu.roll(folded, shift, 1)
    grad_out[...] = folded
    for copy in spread(grad_out, grad_in, grad_s, grad_r, "slab", n, me):
        copy.wait()
    partial = total_of(grad_out[...], grad_in, n, me)
    grad_out2[...] = partial
    for copy in spread(grad_out2, grad_in2, grad2_s, grad2_r, "freq", nf, mine):
        copy.wait()
    gradient_ref[...] = total_of(partial, grad_in2, nf, mine)


def body(source, omega, sigma_blocks, block_ids, rec_owner, rec_edge, observed):
    n, nf = lax.axis_size("slab"), lax.axis_size("freq")
    planes, rows, lanes = block_ids.shape
    blocks = sigma_blocks.shape[0]
    high_blocks = blocks // LOW
    vmem = pl.BlockSpec(memory_space=pltpu.VMEM)
    smem = pl.BlockSpec(memory_space=pltpu.SMEM)
    cell = jax.ShapeDtypeStruct((planes, rows, lanes), F32)
    factor_real, factor_imag = pl.pallas_call(
        lookup_kernel,
        out_shape=(cell, cell),
        in_specs=[smem, vmem, vmem],
        out_specs=(vmem, vmem),
        name="lookup",
    )(omega, sigma_blocks.reshape(-1, lanes), block_ids)
    zero = jnp.zeros((lanes,), F32)
    pack = jnp.stack(
        [
            rec_owner[:, 0].astype(F32),
            (rec_edge >> 7).astype(F32),
            (rec_edge & 127).astype(F32),
            observed[0, 0],
            observed[0, 1],
            zero,
            zero,
            zero,
        ]
    )
    count = sum(1 if i == j else 2 for i, j in PAIRS)
    slots = 2 * SWEEPS
    cells_rows = 3 * planes * rows
    field = jax.ShapeDtypeStruct((2, 3, planes, rows, lanes), F32)
    halo = pltpu.VMEM((slots, 2, 2, rows, lanes), F32)
    dma = pltpu.SemaphoreType.DMA
    grad = pltpu.VMEM((high_blocks, lanes), F32)
    forward, adjoint, gradient = pl.pallas_call(
        functools.partial(kernel, n, nf, high_blocks),
        out_shape=(field, field, jax.ShapeDtypeStruct((high_blocks, lanes), F32)),
        in_specs=[smem, vmem, vmem, vmem, vmem, vmem],
        out_specs=(vmem, vmem, vmem),
        scratch_shapes=[
            pltpu.VMEM((SWEEPS + 1, 2, 3, planes, rows, lanes), F32),
            pltpu.VMEM((2, 3, planes, rows, lanes), F32),
            pltpu.VMEM((2, 2, planes, rows, lanes), F32),
            halo, halo, halo, halo,
            pltpu.VMEM((2, count, lanes), F32),
            pltpu.VMEM((2, n, count, lanes), F32),
            pltpu.VMEM((n, 8, lanes), F32),
            grad,
            pltpu.VMEM((n, high_blocks, lanes), F32),
            grad,
            pltpu.VMEM((nf, high_blocks, lanes), F32),
            pltpu.VMEM((lanes, cells_rows), BF16),
            pltpu.VMEM((cells_rows, n * lanes), BF16),
            pltpu.VMEM((cells_rows, 2 * lanes), BF16),
            pltpu.VMEM((cells_rows, 2 * lanes), BF16),
            pltpu.VMEM((n * lanes, 2 * lanes), BF16),
            pltpu.VMEM((n * lanes, 2 * lanes), BF16),
            pltpu.VMEM((16 * high_blocks, 16 * LOW), F32),
            dma((slots,)), dma((slots,)), dma((slots,)), dma((slots,)),
            dma((2, n)), dma((2, n)),
            dma((n,)), dma((n,)),
            dma((n,)), dma((n,)),
            dma((nf,)), dma((nf,)),
        ],
        compiler_params=pltpu.CompilerParams(
            collective_id=0, has_side_effects=True, vmem_limit_bytes=52 * 1024 * 1024
        ),
        name="solves",
    )(omega, source[0], factor_real, factor_imag, block_ids, pack)
    return forward[None], adjoint[None], gradient[:, :LOW].reshape(blocks)


def solution(mesh):
    return jax.shard_map(
        body,
        mesh=mesh,
        in_specs=(
            P("freq", None, None, "slab", None, None),
            P("freq"),
            P(),
            P("slab", None, None),
            P("slab", None),
            P("slab"),
            P("freq", None, "slab"),
        ),
        out_specs=(
            P("freq", None, None, "slab", None, None),
            P("freq", None, None, "slab", None, None),
            P(),
        ),
        check_vma=False,
    )
```

```python
import functools

import jax
import jax.numpy as jnp
from jax import lax
from jax.experimental import pallas as pl
from jax.experimental.pallas import tpu as pltpu
from jax.sharding import PartitionSpec as P

SWEEPS = 4
EPSILON = 1e-06
LOW = 16
MESH = pl.DeviceIdType.MESH
F32 = jnp.float32
BF16 = jnp.bfloat16
PAIRS = [(i, j) for j in range(1, SWEEPS + 1) for i in range(j + 1)]
WIDTH = SWEEPS


def lookup_kernel(omega_ref, sigma_ref, ids_ref, damping_ref):
    planes, rows, lanes = ids_ref.shape
    tables = [jnp.broadcast_to(sigma_ref[k : k + 1, :], (8, lanes)) for k in range(sigma_ref.shape[0])]
    omega = omega_ref[0]
    per = rows // 8

    def step(i, carry):
        x, y = i // per, pl.multiple_of(i % per * 8, 8)
        ids = ids_ref[x, pl.ds(y, 8), :]
        low, high = ids & (lanes - 1), ids >> 7
        value = jnp.take_along_axis(tables[0], low, axis=1)
        for k in range(1, len(tables)):
            value = jnp.where(high == k, jnp.take_along_axis(tables[k], low, axis=1), value)
        damping_ref[x, pl.ds(y, 8), :] = omega * value
        return carry

    lax.fori_loop(0, planes * per, step, 0, unroll=4)


def split(values):
    high = values.astype(BF16)
    return high, (values - high.astype(F32)).astype(BF16)


def kernel(
    n, nf, high_blocks,
    omega_ref, source_ref, damping_ref, ids_ref, owner_ref, edge_ref, observed_ref,
    forward_ref, adjoint_ref, gradient_ref,
    real_ref, imag_ref, beside, pack_ref, mis_out, mis_in,
    basis, zb, curl, up_out, down_out, low_in, high_in,
    gram_out, gram_in, pack_in, grad_out, grad_in, grad_out2, grad_in2,
    rows_hot, rows_hot_t, field_hi, field_lo, mis_hi, mis_lo, acc,
    up_s, up_r, down_s, down_r, gram_s, gram_r, pack_s, pack_r, grad_s, grad_r, grad2_s, grad2_r,
    near_s, near_r,
):
    me = lax.axis_index("slab")
    mine = lax.axis_index("freq")
    planes, rows, lanes = damping_ref.shape
    first, last = WIDTH, WIDTH + planes - 1
    wide_planes = planes + 2 * WIDTH
    cells_rows = 3 * planes * rows
    wide_rows = 3 * wide_planes * rows

    barrier = pltpu.get_barrier_semaphore()
    for d in range(1, n):
        pl.semaphore_signal(barrier, inc=1, device_id={"slab": lax.rem(me + d, n)}, device_id_type=MESH)
    for d in range(1, nf):
        pl.semaphore_signal(barrier, inc=1, device_id={"freq": lax.rem(mine + d, nf)}, device_id_type=MESH)
    pl.semaphore_wait(barrier, n + nf - 2)

    def spread(src, dst, send, recv, axis, count, position):
        copies = []
        for d in range(1, count):
            copy = pltpu.make_async_remote_copy(
                src_ref=src, dst_ref=dst.at[d], send_sem=send.at[d], recv_sem=recv.at[d],
                device_id={axis: lax.rem(position + d, count)}, device_id_type=MESH,
            )
            copy.start()
            copies.append(copy)
        return copies

    def total_of(own, buffer, count, position):
        buffer[0] = own
        total = jnp.zeros(own.shape, F32)
        for p in range(count):
            total = total + buffer[lax.rem(position - p + count, count)]
        return total

    lane = lax.broadcasted_iota(jnp.int32, (rows, lanes), 1)
    row = lax.broadcasted_iota(jnp.int32, (rows, lanes), 0)

    def f3(v):
        return jnp.where(lane == lanes - 1, 0.0, pltpu.roll(v, lanes - 1, 1)) - v

    def g3(v):
        return jnp.where(lane == 0, 0.0, pltpu.roll(v, 1, 1)) - v

    def f2(v):
        return jnp.where(row == rows - 1, 0.0, pltpu.roll(v, rows - 1, 0)) - v

    def g2(v):
        return jnp.where(row == 0, 0.0, pltpu.roll(v, 1, 0)) - v

    edge = edge_ref[...]
    blank = jnp.zeros((3, lanes), F32)
    pack_ref[...] = jnp.concatenate(
        [owner_ref[...].astype(F32), (edge >> 7).astype(F32), (edge & 127).astype(F32), observed_ref[...], blank],
        axis=0,
    )
    packs = []
    for d in range(1, n):
        copy = pltpu.make_async_remote_copy(
            src_ref=pack_ref, dst_ref=pack_in.at[me], send_sem=pack_s.at[d], recv_sem=pack_r.at[d],
            device_id={"slab": lax.rem(me + d, n)}, device_id_type=MESH,
        )
        copy.start()
        packs.append(copy)
    pack_in[me] = pack_ref[...]
    valid = jnp.where(me > 0, 1.0, 0.0).astype(F32)

    def factors(x, damping):
        inverse = 1.0 / (16.0 + damping * damping)
        real_ref[x] = 4.0 * inverse
        imag_ref[x] = damping * inverse

    def own_factors(x, carry):
        factors(x + first, damping_ref[x])
        for c in range(2):
            for comp in range(3):
                basis[0, c, comp, x + first] = source_ref[c, comp, x].astype(F32)
        return carry

    lax.fori_loop(0, planes, own_factors, 0)

    def beside_copy(side):
        begin, to = (planes - WIDTH, me + 1) if side == 0 else (0, me + n - 1)
        return pltpu.make_async_remote_copy(
            src_ref=damping_ref.at[pl.ds(begin, WIDTH)], dst_ref=beside.at[side], send_sem=near_s.at[side],
            recv_sem=near_r.at[side], device_id={"slab": lax.rem(to, n)}, device_id_type=MESH,
        )

    def misfit_copy(side):
        to = me + 1 if side == 0 else me + n - 1
        return pltpu.make_async_remote_copy(
            src_ref=mis_out, dst_ref=mis_in.at[side], send_sem=near_s.at[2 + side],
            recv_sem=near_r.at[2 + side], device_id={"slab": lax.rem(to, n)}, device_id_type=MESH,
        )

    def precondition(t, x):
        mr, mi = real_ref[x], imag_ref[x]
        for comp in range(3):
            br, bi = basis[t, 0, comp, x], basis[t, 1, comp, x]
            zb[0, comp, x] = mr * br + mi * bi
            zb[1, comp, x] = mr * bi - mi * br

    def up_copy(slot):
        return pltpu.make_async_remote_copy(
            src_ref=up_out.at[slot], dst_ref=low_in.at[slot], send_sem=up_s.at[slot],
            recv_sem=up_r.at[slot], device_id={"slab": lax.rem(me + 1, n)}, device_id_type=MESH,
        )

    def down_copy(slot):
        return pltpu.make_async_remote_copy(
            src_ref=down_out.at[slot], dst_ref=high_in.at[slot], send_sem=down_s.at[slot],
            recv_sem=down_r.at[slot], device_id={"slab": lax.rem(me + n - 1, n)}, device_id_type=MESH,
        )

    def plane(t, c, x, e2n, e3n, b2p, b3p):
        e1, e2, e3 = zb[c, 0, x], zb[c, 1, x], zb[c, 2, x]
        b1 = f2(e3) - f3(e2)
        b2 = f3(e1) - (e3n - e3)
        b3 = e2n - e2 - f2(e1)
        curl[c, 0, x], curl[c, 1, x] = b2, b3
        basis[t + 1, c, 0, x] = g3(b2) - g2(b3) - 4.0 * e1 + basis[t, c, 0, x]
        basis[t + 1, c, 1, x] = b3p - b3 - g3(b1) - 4.0 * e2 + basis[t, c, 1, x]
        basis[t + 1, c, 2, x] = g2(b1) - (b2p - b2) - 4.0 * e3 + basis[t, c, 2, x]

    def lower_curl(x):
        for c in range(2):
            curl[c, 0, x] = f3(zb[c, 0, x]) - (zb[c, 2, x + 1] - zb[c, 2, x])
            curl[c, 1, x] = zb[c, 1, x + 1] - zb[c, 1, x] - f2(zb[c, 0, x])

    def apply(t, meanwhile):
        slot = t
        precondition(t, first)
        for c in range(2):
            down_out[slot, c, 0] = zb[c, 1, first]
            down_out[slot, c, 1] = zb[c, 2, first]

        @pl.when(me > 0)
        def _():
            down_copy(slot).start()

        precondition(t, last)
        for c in range(2):
            up_out[slot, c, 0] = f3(zb[c, 0, last]) + zb[c, 2, last]
            up_out[slot, c, 1] = f2(zb[c, 0, last]) + zb[c, 1, last]

        @pl.when(me < n - 1)
        def _():
            up_copy(slot).start()

        def inner(x, carry):
            precondition(t, x)
            return carry

        lax.fori_loop(first + 1, last, inner, 0)
        lower_curl(first)

        def middle(x, carry):
            for c in range(2):
                plane(t, c, x, zb[c, 1, x + 1], zb[c, 2, x + 1], curl[c, 0, x - 1], curl[c, 1, x - 1])
            return carry

        lax.fori_loop(first + 1, last, middle, 0)
        meanwhile()

        @pl.when(me > 0)
        def _():
            up_copy(slot).wait_recv()
            down_copy(slot).wait_send()

        @pl.when(me == 0)
        def _():
            low_in[slot] = jnp.zeros(low_in.shape[1:], F32)

        for c in range(2):
            plane(
                t, c, first, zb[c, 1, first + 1], zb[c, 2, first + 1],
                (low_in[slot, c, 0] - zb[c, 2, first]) * valid,
                (zb[c, 1, first] - low_in[slot, c, 1]) * valid,
            )

        @pl.when(me < n - 1)
        def _():
            down_copy(slot).wait_recv()
            up_copy(slot).wait_send()

        @pl.when(me == n - 1)
        def _():
            high_in[slot] = jnp.zeros(high_in.shape[1:], F32)

        for c in range(2):
            plane(
                t, c, last, high_in[slot, c, 0], high_in[slot, c, 1],
                curl[c, 0, last - 1], curl[c, 1, last - 1],
            )

    def apply_wide(t):
        def inner(x, carry):
            precondition(t, x)
            return carry

        lax.fori_loop(t, wide_planes - t, inner, 0)
        lower_curl(t)

        def middle(x, carry):
            keep = jnp.where((x == first) & (me == 0), 0.0, 1.0).astype(F32)
            for c in range(2):
                plane(
                    t, c, x, zb[c, 1, x + 1], zb[c, 2, x + 1],
                    curl[c, 0, x - 1] * keep, curl[c, 1, x - 1] * keep,
                )
            return carry

        lax.fori_loop(t + 1, wide_planes - t - 1, middle, 0)

    per = rows // 8

    def solve(which, out_ref):
        def pair_sums(j_):
            width = 2 * j_ + 1

            def products(i, sums):
                x, y = i // per + first, pl.multiple_of(i % per * 8, 8)
                sums = list(sums)
                for comp in range(3):
                    re = [basis[k, 0, comp, x, pl.ds(y, 8), :] for k in range(j_ + 1)]
                    im = [basis[k, 1, comp, x, pl.ds(y, 8), :] for k in range(j_ + 1)]
                    for i_ in range(j_ + 1):
                        sums[2 * i_] = sums[2 * i_] + (re[i_] * re[j_] + im[i_] * im[j_])
                        if i_ != j_:
                            sums[2 * i_ + 1] = sums[2 * i_ + 1] + (re[i_] * im[j_] - im[i_] * re[j_])
                return tuple(sums)

            zero = jnp.zeros((8, lanes), F32)
            sums = lax.fori_loop(0, planes * per, products, (zero,) * width, unroll=2)
            for k in range(width):
                at = j_ * j_ - 1 + k
                gram_out[which, at : at + 1, :] = jnp.sum(sums[k], axis=0, keepdims=True)

        for t in range(SWEEPS):
            if which == 0:
                apply(t, functools.partial(pair_sums, t) if t else lambda: None)
            else:
                apply_wide(t)
                if t:
                    pair_sums(t)
        pair_sums(SWEEPS)
        copies = spread(gram_out.at[which], gram_in.at[which], gram_s.at[which], gram_r.at[which], "slab", n, me)
        for copy in copies:
            copy.wait()
        if which == 0:
            @pl.when(me > 0)
            def _():
                beside_copy(1).start()

            @pl.when(me < n - 1)
            def _():
                beside_copy(0).start()
        total = total_of(gram_out[which], gram_in.at[which], n, me)
        total = jnp.broadcast_to(jnp.sum(total, axis=1, keepdims=True), total.shape)
        gram, at = {}, 0
        for i, j in PAIRS:
            re = total[at : at + 1, :]
            at += 1
            im = jnp.zeros_like(re)
            if i != j:
                im = total[at : at + 1, :]
                at += 1
            gram[i, j] = (re, im)
            gram[j, i] = (re, -im)
        one = jnp.ones((1, lanes), F32)
        none = jnp.zeros((1, lanes), F32)

        def times(a, b):
            return a[0] * b[0] - a[1] * b[1], a[0] * b[1] + a[1] * b[0]

        poly = [(one, none)]
        coef = [(none, none) for _ in range(SWEEPS)]
        for k in range(SWEEPS):
            up = (none, none)
            below = none
            for i in range(k + 1):
                conj = (poly[i][0], -poly[i][1])
                for j in range(k + 1):
                    both = times(conj, poly[j])
                    term = times(both, gram[i + 1, j])
                    up = (up[0] + term[0], up[1] + term[1])
                    below = below + times(both, gram[i + 1, j + 1])[0]
            below = below + EPSILON
            step = (up[0] / below, up[1] / below)
            moved = [times(step, p) for p in poly]
            for i in range(k + 1):
                coef[i] = (coef[i][0] + moved[i][0], coef[i][1] + moved[i][1])
            grown = poly + [(none, none)]
            for i in range(k + 1):
                grown[i + 1] = (grown[i + 1][0] - moved[i][0], grown[i + 1][1] - moved[i][1])
            poly = grown

        wide = [(jnp.broadcast_to(a, (rows, lanes)), jnp.broadcast_to(b, (rows, lanes))) for a, b in coef]

        def combine(x, carry):
            mr, mi = real_ref[x + first], imag_ref[x + first]
            for comp in range(3):
                sr = jnp.zeros((rows, lanes), F32)
                si = jnp.zeros((rows, lanes), F32)
                for k in range(SWEEPS):
                    br, bi = basis[k, 0, comp, x + first], basis[k, 1, comp, x + first]
                    sr = sr + (wide[k][0] * br - wide[k][1] * bi)
                    si = si + (wide[k][0] * bi + wide[k][1] * br)
                out_ref[0, comp, x] = mr * sr + mi * si
                out_ref[1, comp, x] = mr * si - mi * sr
            return carry

        lax.fori_loop(0, planes, combine, 0)

    solve(0, forward_ref)

    for copy in packs:
        copy.wait()
    self_id = me.astype(F32)
    blocks = cells_rows // lanes
    wide_blocks = wide_rows // lanes
    for comp in range(3):
        for c in range(2):
            hi, lo = split(forward_ref[c, comp].reshape(planes * rows, lanes))
            where = (slice(comp * planes * rows, (comp + 1) * planes * rows), slice(c * lanes, (c + 1) * lanes))
            field_hi[where] = hi
            field_lo[where] = lo

    lane_sq = lax.broadcasted_iota(jnp.int32, (lanes, lanes), 1).astype(F32)
    row_sq = lax.broadcasted_iota(jnp.int32, (lanes, lanes), 0).astype(F32)

    def receivers(d, carry):
        pack = pack_in[d]
        at = pl.ds(pl.multiple_of(d * lanes, lanes), lanes)
        owned = jnp.where(pack[0:1, :] == self_id, pack[1:2, :], -1.0)
        owned = jnp.concatenate([owned, pack[2:8, :], owned], axis=0)
        column = jnp.concatenate([owned] * (lanes // 8), axis=0).T
        place = column[:, 0:1]
        for k in range(blocks):
            rows_hot[:, k * lanes : (k + 1) * lanes] = jnp.where(
                lane_sq == place - float(k * lanes), 1.0, 0.0
            ).astype(BF16)
        picked = jnp.dot(rows_hot[...], field_hi[...], preferred_element_type=F32)
        picked = picked + jnp.dot(rows_hot[...], field_lo[...], preferred_element_type=F32)
        here = (lane_sq == column[:, 1:2]) & (place >= 0.0)
        re = jnp.where(here, picked[:, :lanes] - column[:, 2:3], 0.0)
        im = jnp.where(here, column[:, 3:4] - picked[:, lanes:], 0.0)
        both = jnp.where(
            lane_sq == 0.0,
            jnp.sum(re, axis=1, keepdims=True),
            jnp.where(lane_sq == 1.0, jnp.sum(im, axis=1, keepdims=True), 0.0),
        )
        mis_out[d] = both.T[0:8, :]
        return carry

    lax.fori_loop(0, n, receivers, 0)

    @pl.when(me > 0)
    def _():
        misfit_copy(1).start()

    @pl.when(me < n - 1)
    def _():
        misfit_copy(0).start()

    def places(p, carry):
        at = pl.ds(pl.multiple_of(p * lanes, lanes), lanes)
        pack = pack_in[p]
        apart = pack[0:1, :] - self_id
        number = pack[1:2, :].astype(jnp.int32)
        comp = jnp.where(number >= 2 * planes * rows, 2, jnp.where(number >= planes * rows, 1, 0))
        offset = (apart * float(planes * rows)).astype(jnp.int32) + WIDTH * rows
        inside = number - comp * (planes * rows) + offset
        fits = (inside >= 0) & (inside < wide_planes * rows)
        spot = jnp.where(fits, inside + comp * (wide_planes * rows), -1).astype(F32)
        for k in range(wide_blocks):
            rows_hot_t[k * lanes : (k + 1) * lanes, at] = jnp.where(
                row_sq == spot - float(k * lanes), 1.0, 0.0
            ).astype(BF16)
        return carry

    lax.fori_loop(0, n, places, 0)

    @pl.when(me > 0)
    def _():
        misfit_copy(0).wait_recv()
        misfit_copy(1).wait_send()
        beside_copy(0).wait_recv()
        beside_copy(1).wait_send()

    @pl.when(me < n - 1)
    def _():
        misfit_copy(1).wait_recv()
        misfit_copy(0).wait_send()
        beside_copy(1).wait_recv()
        beside_copy(0).wait_send()

    for side, there in enumerate((me > 0, me < n - 1)):
        start = 0 if side == 0 else last + 1

        @pl.when(there)
        def _(side=side, start=start):
            for k in range(WIDTH):
                factors(start + k, beside[side, k])

        @pl.when(jnp.logical_not(there))
        def _(side=side, start=start):
            mis_in[side] = jnp.zeros(mis_in.shape[1:], F32)
            for k in range(WIDTH):
                real_ref[start + k] = jnp.zeros((rows, lanes), F32)
                imag_ref[start + k] = jnp.zeros((rows, lanes), F32)

    def values_of(p, carry):
        at = pl.ds(pl.multiple_of(p * lanes, lanes), lanes)
        value = mis_out[p] + mis_in[0, p] + mis_in[1, p]
        value = jnp.concatenate([value[0:2, :], pack_in[p][2:8, :]], axis=0)
        column = jnp.concatenate([value] * (lanes // 8), axis=0).T
        here = lane_sq == column[:, 2:3]
        for part in range(2):
            hi, lo = split(jnp.where(here, column[:, part : part + 1], 0.0))
            mis_hi[at, part * lanes : (part + 1) * lanes] = hi
            mis_lo[at, part * lanes : (part + 1) * lanes] = lo
        return carry

    lax.fori_loop(0, n, values_of, 0)
    group = 4
    for comp in range(3):
        for x in range(0, wide_planes, group):
            begin = (comp * wide_planes + x) * rows
            hot = rows_hot_t[begin : begin + group * rows, :]
            added = jnp.dot(hot, mis_hi[...], preferred_element_type=F32)
            added = added + jnp.dot(hot, mis_lo[...], preferred_element_type=F32)
            for c in range(2):
                basis[0, c, comp, x : x + group] = added[:, c * lanes : (c + 1) * lanes].reshape(
                    group, rows, lanes
                )

    solve(1, adjoint_ref)

    omega = omega_ref[0]
    high_iota = lax.broadcasted_iota(jnp.int32, (high_blocks, lanes), 0)
    low_iota = lax.broadcasted_iota(jnp.int32, (LOW, lanes), 0)
    acc[...] = jnp.zeros(acc.shape, F32)
    chunks = rows // 16

    def cells(i, carry):
        x, y = i // chunks, pl.multiple_of(i % chunks * 16, 16)
        value = jnp.zeros((16, lanes), F32)
        for comp in range(3):
            fr, fi = forward_ref[0, comp, x, pl.ds(y, 16), :], forward_ref[1, comp, x, pl.ds(y, 16), :]
            ar, ai = adjoint_ref[0, comp, x, pl.ds(y, 16), :], adjoint_ref[1, comp, x, pl.ds(y, 16), :]
            value = value + (ar * fi + ai * fr)
        value = omega * value
        ids = ids_ref[x, pl.ds(y, 16), :]
        high, low = ids >> 4, ids & (LOW - 1)
        hot = jnp.concatenate(
            [jnp.where(high[r : r + 1, :] == high_iota, 1.0, 0.0) for r in range(16)], axis=0
        ).astype(BF16)
        spot = jnp.concatenate(
            [jnp.where(low[r : r + 1, :] == low_iota, value[r : r + 1, :], 0.0) for r in range(16)], axis=0
        )
        acc[...] += lax.dot_general(
            jnp.concatenate([hot, hot], axis=1), jnp.concatenate(split(spot), axis=1),
            (((1,), (1,)), ((), ())), preferred_element_type=F32,
        )
        return carry

    lax.fori_loop(0, planes * chunks, cells, 0)
    wide_lane = lax.broadcasted_iota(jnp.int32, (high_blocks, 16 * LOW), 1)
    diagonal = jnp.zeros((high_blocks, 16 * LOW), F32)
    for r in range(16):
        inside = (wide_lane >= r * LOW) & (wide_lane < (r + 1) * LOW)
        diagonal = diagonal + jnp.where(inside, acc[r * high_blocks : (r + 1) * high_blocks, :], 0.0)
    folded = diagonal[:, :lanes] + diagonal[:, lanes:]
    for shift in (64, 32, 16):
        folded = folded + pltpu.roll(folded, shift, 1)
    grad_out[...] = folded
    for copy in spread(grad_out, grad_in, grad_s, grad_r, "slab", n, me):
        copy.wait()
    partial = total_of(grad_out[...], grad_in, n, me)
    grad_out2[...] = partial
    for copy in spread(grad_out2, grad_in2, grad2_s, grad2_r, "freq", nf, mine):
        copy.wait()
    gradient_ref[...] = total_of(partial, grad_in2, nf, mine)


def body(source, omega, sigma_blocks, block_ids, rec_owner, rec_edge, observed):
    n, nf = lax.axis_size("slab"), lax.axis_size("freq")
    planes, rows, lanes = block_ids.shape
    blocks = sigma_blocks.shape[0]
    high_blocks = blocks // LOW
    vmem = pl.BlockSpec(memory_space=pltpu.VMEM)
    smem = pl.BlockSpec(memory_space=pltpu.SMEM)
    cell = jax.ShapeDtypeStruct((planes, rows, lanes), F32)
    damping = pl.pallas_call(
        lookup_kernel,
        out_shape=cell,
        in_specs=[smem, vmem, vmem],
        out_specs=vmem,
        name="lookup",
    )(omega, sigma_blocks.reshape(-1, lanes), block_ids)
    count = sum(1 if i == j else 2 for i, j in PAIRS)
    slots = SWEEPS
    cells_rows = 3 * planes * rows
    wide_planes = planes + 2 * WIDTH
    field = jax.ShapeDtypeStruct((2, 3, planes, rows, lanes), F32)
    halo = pltpu.VMEM((slots, 2, 2, rows, lanes), F32)
    dma = pltpu.SemaphoreType.DMA
    grad = pltpu.VMEM((high_blocks, lanes), F32)
    forward, adjoint, gradient = pl.pallas_call(
        functools.partial(kernel, n, nf, high_blocks),
        out_shape=(field, field, jax.ShapeDtypeStruct((high_blocks, lanes), F32)),
        in_specs=[smem] + [vmem] * 6,
        out_specs=(vmem, vmem, vmem),
        scratch_shapes=[
            pltpu.VMEM((wide_planes, rows, lanes), F32),
            pltpu.VMEM((wide_planes, rows, lanes), F32),
            pltpu.VMEM((2, WIDTH, rows, lanes), F32),
            pltpu.VMEM((8, lanes), F32),
            pltpu.VMEM((n, 8, lanes), F32),
            pltpu.VMEM((2, n, 8, lanes), F32),
            pltpu.VMEM((SWEEPS + 1, 2, 3, wide_planes, rows, lanes), F32),
            pltpu.VMEM((2, 3, wide_planes, rows, lanes), F32),
            pltpu.VMEM((2, 2, wide_planes, rows, lanes), F32),
            halo, halo, halo, halo,
            pltpu.VMEM((2, count, lanes), F32),
            pltpu.VMEM((2, n, count, lanes), F32),
            pltpu.VMEM((n, 8, lanes), F32),
            grad,
            pltpu.VMEM((n, high_blocks, lanes), F32),
            grad,
            pltpu.VMEM((nf, high_blocks, lanes), F32),
            pltpu.VMEM((lanes, cells_rows), BF16),
            pltpu.VMEM((3 * wide_planes * rows, n * lanes), BF16),
            pltpu.VMEM((cells_rows, 2 * lanes), BF16),
            pltpu.VMEM((cells_rows, 2 * lanes), BF16),
            pltpu.VMEM((n * lanes, 2 * lanes), BF16),
            pltpu.VMEM((n * lanes, 2 * lanes), BF16),
            pltpu.VMEM((16 * high_blocks, 16 * LOW), F32),
            dma((slots,)), dma((slots,)), dma((slots,)), dma((slots,)),
            dma((2, n)), dma((2, n)),
            dma((n,)), dma((n,)),
            dma((n,)), dma((n,)),
            dma((nf,)), dma((nf,)),
            dma((4,)), dma((4,)),
        ],
        compiler_params=pltpu.CompilerParams(
            collective_id=0, has_side_effects=True, vmem_limit_bytes=52 * 1024 * 1024
        ),
        name="solves",
    )(
        omega, source[0], damping, block_ids,
        rec_owner.reshape(1, -1), rec_edge.reshape(1, -1), observed[0],
    )
    return forward[None], adjoint[None], gradient[:, :LOW].reshape(blocks)


def solution(mesh):
    return jax.shard_map(
        body,
        mesh=mesh,
        in_specs=(
            P("freq", None, None, "slab", None, None),
            P("freq"),
            P(),
            P("slab", None, None),
            P("slab", None),
            P("slab"),
            P("freq", None, "slab"),
        ),
        out_specs=(
            P("freq", None, None, "slab", None, None),
            P("freq", None, None, "slab", None, None),
            P(),
        ),
        check_vma=False,
    )
```
